128 devices in a mesh: cube: 8 (over x_hi, z), front: 16 (over y, x_lo, core).
Axes of the slice: x: 4 (x_hi: 2, x_lo: 2; x = x_hi * 2 + x_lo), y: 4, z: 4, core: 2. Of those that a mesh axis runs over, the one named last changes fastest.
Arguments:
- child_block: float32 [8, 16, 14, 128, 512], P('cube', 'front'), may hold values from -4 to 4, as said below
- child_rows: int32 [8, 16, 14], P('cube', 'front'), may hold values from 0 to 255, as said below
- child_cols: int32 [8, 4], P('cube'), may hold values from 0 to 5, as said below
- parent_base: float32 [8, 16, 8, 128, 768], P('cube', 'front'), may hold values from -16 to 36, as said below
Outputs:
- lower_factor: float32 [8, 16, 8, 128, 768], P('cube', 'front')
The draws below stay inside these ranges and needn't reach their ends.
Inputs may be any that keep to these rules, and one draw needn't show every extreme that they name: `child_rows`: group g's child feeds the front of pair g // 2. The 14 tiles at front index f go to distinct increasing parent tiles within 2 * 16 * (f % 8) to 2 * 16 * (f % 8 + 1) - 1; each child's first tile goes to 0 and its last to 255. `child_cols`: distinct and increasing for each group; the first is 0 and the last 5. `child_block`: rows of tiles that go to parent tiles under 6 lie within -0.005 to 0.005. `parent_base`: the first 768 rows of each front form a symmetric matrix whose smallest eigenvalue is 10 or more.
All inputs are finite; a program needn't handle non-finite values.
Results may differ from the reference program's by a relative error of at most 0.0001.
Values sent between devices are 32-bit elements; how exact they have to be, the bound alone decides.
A program may use at most 128 MiB of HBM per device.

```python
import jax
import jax.numpy as jnp
from jax import lax

TILE = 128
PANEL = 256
NPAN = 3
RT = 8
TPD = 14
CT = 4
WT = 6
WC = 768
N_CUBE = 8
N_FRONT = 16


def tile_targets(key):
    run_span = 2 * N_FRONT
    subkeys = jax.random.split(key, N_CUBE * N_FRONT)
    shuffled = jax.vmap(lambda subkey: jax.random.permutation(subkey, run_span))(subkeys)
    picked = jnp.sort(shuffled[:, :TPD], axis=1).reshape(N_CUBE, N_FRONT, TPD)
    run_ids = jnp.arange(N_FRONT, dtype=jnp.int32) % RT
    offsets = (run_span * run_ids)[None, :, None]
    targets = (picked + offsets).astype(jnp.int32)
    targets = targets.at[:, 0, 0].set(0)
    targets = targets.at[:, N_FRONT - 1, TPD - 1].set(run_span * RT - 1)
    return targets


def draw_child_rows(key, part):
    return tile_targets(key)


def draw_child_cols(key, part):
    key = jax.random.fold_in(key, 11)
    subkeys = jax.random.split(key, N_CUBE)
    shuffled = jax.vmap(lambda subkey: jax.random.permutation(subkey, WT - 2))(subkeys)
    middle = jnp.sort(shuffled[:, :CT - 2], axis=1).astype(jnp.int32) + 1
    first_col = jnp.zeros((N_CUBE, 1), jnp.int32)
    last_col = jnp.full((N_CUBE, 1), WT - 1, jnp.int32)
    return jnp.concatenate([first_col, middle, last_col], axis=1)


def draw_child_block(key, part):
    targets = tile_targets(key)
    key = jax.random.fold_in(key, 7)
    first_key, second_key = jax.random.split(key, 2)
    shape = (N_CUBE, N_FRONT, TPD, TILE, CT * TILE)
    leading = (targets < WT)[:, :, :, None, None]
    small_part = jax.random.uniform(first_key, shape, jnp.float32, -0.005, 0.005)
    rest = jnp.clip(jax.random.normal(second_key, shape, jnp.float32), -4.0, 4.0)
    return jnp.where(leading, small_part, rest)


def draw_parent_base(key, part):
    key = jax.random.fold_in(key, 5)
    shape = (N_CUBE, N_FRONT, RT, TILE, WC)
    row_shape = shape[:4]
    group = lax.broadcasted_iota(jnp.int32, row_shape, 0)
    front_ix = lax.broadcasted_iota(jnp.int32, row_shape, 1)
    slot_ix = lax.broadcasted_iota(jnp.int32, row_shape, 2)
    row_ix = lax.broadcasted_iota(jnp.int32, row_shape, 3)
    global_row = (slot_ix * (2 * N_FRONT) + 2 * front_ix + group % 2) * TILE + row_ix
    first_key, second_key, third_key = jax.random.split(key, 3)
    pair_count = N_CUBE // 2
    coupling = jax.random.randint(first_key, (pair_count, WC, WC), -2, 3).astype(jnp.float32)
    gram_part = jnp.einsum('pik,pjk->pij', coupling, coupling, precision=lax.Precision.HIGHEST) * (4.0 / WC)
    levels = jax.random.uniform(second_key, (pair_count, WC), jnp.float32)
    diag_shift = 10.0 + 10.0 * levels
    rest = jnp.clip(jax.random.normal(third_key, shape, jnp.float32), -4.0, 4.0)
    identity = jnp.eye(WC, dtype=jnp.float32)
    leading_block = gram_part + diag_shift[:, :, None] * identity[None]
    pair_ix = group // 2
    row_clip = jnp.minimum(global_row, WC - 1)
    lead_vals = leading_block[pair_ix, row_clip]
    leading = (global_row < WC)[..., None]
    return jnp.where(leading, lead_vals, rest)


def setup_inputs(seed: int = 0) -> dict:
    streams_of = jax.random.split(jax.random.key(seed), 5)
    return {
        "child_block": draw_child_block(jax.random.fold_in(streams_of[4], 71), 0),
        "child_rows": draw_child_rows(jax.random.fold_in(streams_of[4], 71), 0),
        "child_cols": draw_child_cols(jax.random.fold_in(streams_of[4], 71), 0),
        "parent_base": draw_parent_base(jax.random.fold_in(streams_of[4], 71), 0),
    }


def widen_cols(child_data, col_map, win_tiles):
    leading = child_data.shape[:-1]
    col_tiles = col_map.shape[0]
    tile_rows = child_data.shape[-2]
    placer = (col_map[:, None] == jnp.arange(win_tiles, dtype=jnp.int32)[None, :]).astype(jnp.float32)
    split_cols = child_data.reshape(leading + (col_tiles, tile_rows))
    widened = jnp.einsum('...cq,cw->...wq', split_cols, placer, precision=lax.Precision.HIGHEST)
    return widened.reshape(leading + (win_tiles * tile_rows,))

def reference(child_block, child_rows, child_cols, parent_base):
    pair_count = N_CUBE // 2
    tile_count = 2 * RT * N_FRONT
    fronts_all = parent_base.reshape(pair_count, 2, N_FRONT, RT, TILE, WC).transpose(0, 3, 2, 1, 4, 5).reshape(pair_count, tile_count, TILE, WC)
    results = []
    for pair_id in range(pair_count):
        front_mat = fronts_all[pair_id]
        for side_bit in range(2):
            group = 2 * pair_id + side_bit
            child_data = child_block[group].reshape(N_FRONT * TPD, TILE, CT * TILE)
            widened = widen_cols(child_data, child_cols[group], WT)
            front_mat = front_mat.at[child_rows[group].reshape(-1)].add(widened)
        assembled = front_mat.reshape(tile_count * TILE, WC)
        for panel_id in range(NPAN):
            col_start = panel_id * PANEL
            col_stop = col_start + PANEL
            factor = jnp.linalg.cholesky(assembled[col_start:col_stop, col_start:col_stop])
            below = lax.linalg.triangular_solve(factor, assembled[col_stop:, col_start:col_stop], left_side=False, lower=True, transpose_a=True)
            assembled = assembled.at[:col_start, col_start:col_stop].set(0.0)
            assembled = assembled.at[col_start:col_stop, col_start:col_stop].set(factor)
            assembled = assembled.at[col_stop:, col_start:col_stop].set(below)
            if col_stop < WC:
                update = jnp.dot(below, below[:WC - col_stop].T, precision=lax.Precision.HIGHEST)
                assembled = assembled.at[col_stop:, col_stop:].add(-update)
        results.append(assembled.reshape(tile_count, TILE, WC))
    stacked = jnp.stack(results).reshape(pair_count, RT, N_FRONT, 2, TILE, WC).transpose(0, 3, 2, 1, 4, 5)
    return stacked.reshape(N_CUBE, N_FRONT, RT, TILE, WC)
```

```python
import functools

import jax
import jax.numpy as jnp
from jax import lax
from jax.experimental import pallas as pl
from jax.experimental.pallas import tpu as pltpu
from jax.sharding import Mesh
from jax.sharding import PartitionSpec as P

MESH = pl.DeviceIdType.MESH
HI = lax.Precision.HIGHEST
VM = pl.BlockSpec(memory_space=pltpu.VMEM)
ANY = pl.BlockSpec(memory_space=pl.ANY)
def nt(a,b,prec=HI):
    return lax.dot_general(a,b,(((1,),(1,)),((),())),precision=prec,preferred_element_type=jnp.float32)
def nn(a,b,prec=HI):
    return lax.dot_general(a,b,(((1,),(0,)),((),())),precision=prec,preferred_element_type=jnp.float32)
def bc(x): return jnp.broadcast_to(x,(8,128))
def base(block):
    sub=lax.broadcasted_iota(jnp.int32,(8,128),0); lane=lax.broadcasted_iota(jnp.int32,(8,128),1)
    S=[block[8*t:8*t+8] for t in range(16)]
    T=[jnp.where(lane==sub+8*t,1.0,0.0).astype(jnp.float32) for t in range(16)]
    U=[];M=[]
    for s in range(16):
        ur=[];mr=[]
        for r in range(0,8,2):
            i=8*s+r
            R=S[s]; Q=T[s]
            c0=bc(R[:,i:i+1]); c1=bc(R[:,i+1:i+2])
            a=bc(c0[r:r+1]); b=bc(c0[r+1:r+2]); c=bc(c1[r+1:r+2])
            w0=bc(R[r:r+1]); w1=bc(R[r+1:r+2]); t0=bc(Q[r:r+1]); t1=bc(Q[r+1:r+2])
            rd=1.0/(a*c-b*b)
            A=c*rd; B=b*rd; C=a*rd
            for t in range(s,16):
                if t>s:
                    c0=bc(S[t][:,i:i+1]); c1=bc(S[t][:,i+1:i+2])
                elif r==6: continue
                else:
                    keep=sub>r+1
                    c0=jnp.where(keep,c0,0.0); c1=jnp.where(keep,c1,0.0)
                e0=c0*A-c1*B; e1=c1*C-c0*B
                S[t]=S[t]-(e0*w0+e1*w1)
                T[t]=T[t]-(e0*t0+e1*t1)
            ra=lax.rsqrt(a); q=b*(ra*ra); rs=lax.rsqrt(c-b*q)
            ur+=[w0*ra,(w1-q*w0)*rs]; mr+=[t0*ra,(t1-q*t0)*rs]
        def merge(rows):
            o=rows[7]
            for k in range(7): o=jnp.where(sub==k,rows[k],o)
            return o
        U.append(merge(ur)); M.append(merge(mr))
    return jnp.concatenate(U,0), jnp.concatenate(M,0)
NB=6
def chol_kernel(a_ref, l_ref, m_ref, w_ref):
    def blk(i,j): return (pl.ds(128*i,128),pl.ds(128*j,128))
    for i in range(NB):
        for j in range(i+1):
            v=a_ref[blk(i,j)]
            if i//2==j//2:
                v=0.5*(v+(v.T if i==j else a_ref[blk(j,i)].T))
            w_ref[blk(i,j)]=v
    tri=lax.broadcasted_iota(jnp.int32,(128,128),0)>=lax.broadcasted_iota(jnp.int32,(128,128),1)
    zero=jnp.zeros((128,128),jnp.float32)
    for k in range(NB):
        U,M=base(w_ref[blk(k,k)])
        l_ref[blk(k,k)]=jnp.where(tri,U.T,0.0)
        m_ref[blk(k,k)]=M
        for j in range(k+1,NB):
            l_ref[blk(k,j)]=zero; m_ref[blk(k,j)]=zero
        if k+1<NB:
            n=128*(NB-1-k); r0=128*(k+1)
            P=nt(w_ref[pl.ds(r0,n),pl.ds(128*k,128)],M)
            l_ref[pl.ds(r0,n),pl.ds(128*k,128)]=P
            for j in range(k+1,NB):
                q0=128*(j-k-1)
                w_ref[pl.ds(128*j,n-q0),pl.ds(128*j,128)]-=nt(P[q0:],P[q0:q0+128])
        if k>0:
            acc=nn(l_ref[pl.ds(128*k,128),pl.ds(0,128*k)],m_ref[pl.ds(0,128*k),pl.ds(0,128*k)])
            m_ref[pl.ds(128*k,128),pl.ds(0,128*k)]=-nn(M,acc)
def chol(top):
    s = jax.ShapeDtypeStruct((768, 768), jnp.float32)
    return pl.pallas_call(
        chol_kernel,
        out_shape=(s, s),
        in_specs=[VM],
        out_specs=(VM, VM),
        scratch_shapes=[pltpu.VMEM((768, 768), jnp.float32)],
        compiler_params=pltpu.CompilerParams(vmem_limit_bytes=40 << 20),
        cost_estimate=pl.CostEstimate(flops=40_000_000_000, bytes_accessed=8_000_000, transcendentals=0),
        name="lead_factor",
    )(top)


def pack_kernel(pick, x_ref, o_ref):
    d = pl.program_id(0)
    o_ref[...] = jnp.where(pick[d] > 0, x_ref[...], 0.0)


def pack(pick, tiles):
    block = (1, 128, 512)
    return pl.pallas_call(
        pack_kernel,
        out_shape=jax.ShapeDtypeStruct((32, 128, 512), jnp.float32),
        grid_spec=pltpu.PrefetchScalarGridSpec(
            num_scalar_prefetch=1,
            grid=(32,),
            in_specs=[pl.BlockSpec(block, lambda d, pick: (jnp.maximum(pick[d] - 1, 0), 0, 0))],
            out_specs=pl.BlockSpec(block, lambda d, pick: (d, 0, 0)),
        ),
        name="pack_tiles",
    )(pick, tiles)


def spread(w, g, s, col):
    if col == 0:
        return s(0)
    if col == 5:
        return s(3)
    if col == 1:
        return s(1) * w[g, 0:1]
    if col == 2:
        return s(1) * w[g, 1:2] + s(2) * w[g, 2:3]
    if col == 3:
        return s(1) * w[g, 3:4] + s(2) * w[g, 4:5]
    return s(2) * w[g, 5:6]


def top_kernel(packed, base_tiles, w_in, top, wb, cbuf, bbuf, ssem, wsem, csem, bsem, ysem, xsem, ksem):
    pair = lax.axis_index("pair")
    z = lax.axis_index("bit")
    f = lax.axis_index("front")
    y, x, k = f // 4, (f // 2) % 2, f % 2

    def at(dz, dy, dx, dk):
        return (pair, (z + dz) % 2, ((y + dy) % 4) * 4 + ((x + dx) % 2) * 2 + (k + dk) % 2)

    bar = pltpu.get_barrier_semaphore()
    for n in range(1, 32):
        pl.semaphore_signal(bar, inc=1, device_id=at(n // 16, (n // 4) % 4, (n // 2) % 2, n % 2), device_id_type=MESH)
    pl.semaphore_wait(bar, 31)

    wb[z] = w_in[...]
    wcopy = pltpu.make_async_remote_copy(
        src_ref=w_in, dst_ref=wb.at[z], send_sem=wsem.at[0], recv_sem=wsem.at[1],
        device_id=at(1, 0, 0, 0), device_id_type=MESH)
    wcopy.start()
    owner = f <= 2
    source = (f == 0) | (f == 8)
    me = z * 2 + y // 2
    widths = (256, 384, 512)

    def child(b, q, remote):
        src = packed.at[b * 16 + q, :, pl.ds(0, widths[q])]
        dst = cbuf.at[me, :, pl.ds(0, widths[q])]
        if remote:
            return pltpu.make_async_remote_copy(
                src_ref=src, dst_ref=dst, send_sem=ssem.at[b * 3 + q], recv_sem=csem.at[me],
                device_id=(pair, b, q), device_id_type=MESH)
        return pltpu.make_async_copy(src, dst, csem.at[me])

    def each(fn):
        for q in range(3):
            for b in range(2):
                if q == 0:
                    own = (f == 0) & (z == b)
                    fn(b, q, source & jnp.logical_not(own), True)
                    if fn is begin:
                        fn(b, q, source & own, False)
                else:
                    fn(b, q, source, True)

    def begin(b, q, cond, remote):
        @pl.when(cond)
        def _():
            child(b, q, remote).start()

    def sent(b, q, cond, remote):
        @pl.when(cond)
        def _():
            child(b, q, remote).wait_send()

    base_copy = pltpu.make_async_copy(base_tiles.at[0, 0, 0], bbuf, bsem)

    @pl.when(owner)
    def _():
        base_copy.start()

    each(begin)
    wcopy.wait_recv()

    p_own = 2 * f + z
    for q in range(3):
        n = widths[q]

        @pl.when(f == q)
        def _(q=q, n=n):
            base_copy.wait()
            for s in range(4):
                pltpu.make_async_copy(packed.at[0, :, pl.ds(0, n)], cbuf.at[s, :, pl.ds(0, n)], csem.at[s]).wait()
            for col in range(2 * q + 2):
                v = bbuf[:, 128 * col:128 * col + 128]
                for g in range(2):
                    v = v + spread(wb, g, lambda c, g=g: cbuf[2 * g, :, 128 * c:128 * c + 128] + cbuf[2 * g + 1, :, 128 * c:128 * c + 128], col)
                top[p_own, :, 128 * col:128 * col + 128] = v

    def tile_copy(q, zz, send, recv, to):
        piece = (2 * q + zz, slice(None), pl.ds(0, 256 * q + 256))
        return pltpu.make_async_remote_copy(
            src_ref=top.at[piece], dst_ref=top.at[piece], send_sem=send, recv_sem=recv, device_id=to, device_id_type=MESH)

    mine = f % 4
    for q in range(3):
        @pl.when(mine == q)
        def _(q=q):
            @pl.when(y == 0)
            def _():
                for n, dy in enumerate((2, 1, 3)):
                    tile_copy(q, z, ssem.at[6 + n], ysem.at[0], at(0, dy, 0, 0)).start()

            @pl.when(y > 0)
            def _():
                tile_copy(q, z, ssem.at[6], ysem.at[0], at(0, 1, 0, 0)).wait_recv()

            for n, (dz, dx) in enumerate(((1, 1), (0, 1), (1, 0))):
                tile_copy(q, z, ssem.at[9 + n], xsem.at[2 * q + z], at(dz, 0, dx, 0)).start()
            tile_copy(q, z, ssem.at[(14 if q == 2 else 12) + z], ksem.at[2 * q + z], at(0, 0, 0, 1)).start()

    for q in range(3):
        @pl.when(k == q % 2)
        def _(q=q):
            for zz in range(2):
                @pl.when((mine != q) | (z != zz))
                def _(zz=zz):
                    tile_copy(q, zz, ssem.at[9], xsem.at[2 * q + zz], at(0, 0, 1, 0)).wait_recv()
                    tile_copy(q, zz, ssem.at[14 + zz if q == 2 else 12 + zz], ksem.at[2 * q + zz], at(0, 0, 0, 1)).start()
    for q in range(3):
        @pl.when(k != q % 2)
        def _(q=q):
            for zz in range(2):
                tile_copy(q, zz, ssem.at[9], ksem.at[2 * q + zz], at(0, 0, 0, 1)).wait_recv()

    wcopy.wait_send()
    each(sent)
    for q in range(3):
        @pl.when(mine == q)
        def _(q=q):
            @pl.when(y == 0)
            def _():
                for n in range(3):
                    tile_copy(q, z, ssem.at[6 + n], ysem.at[0], at(0, 1, 0, 0)).wait_send()

            for n in range(3):
                tile_copy(q, z, ssem.at[9 + n], xsem.at[2 * q + z], at(0, 0, 1, 0)).wait_send()

        @pl.when(k == q % 2)
        def _(q=q):
            for zz in range(2):
                tile_copy(q, zz, ssem.at[14 + zz if q == 2 else 12 + zz], ksem.at[2 * q + zz], at(0, 0, 0, 1)).wait_send()


def lead(packed, base_tiles, w):
    return pl.pallas_call(
        top_kernel,
        out_shape=(jax.ShapeDtypeStruct((6, 128, 768), jnp.float32), jax.ShapeDtypeStruct((2, 8, 128), jnp.float32)),
        in_specs=[ANY, ANY, VM],
        out_specs=(VM, VM),
        scratch_shapes=[
            pltpu.VMEM((4, 128, 512), jnp.float32),
            pltpu.VMEM((128, 768), jnp.float32),
            pltpu.SemaphoreType.DMA((16,)),
            pltpu.SemaphoreType.DMA((2,)),
            pltpu.SemaphoreType.DMA((4,)),
            pltpu.SemaphoreType.DMA,
            pltpu.SemaphoreType.DMA((1,)),
            pltpu.SemaphoreType.DMA((6,)),
            pltpu.SemaphoreType.DMA((6,)),
        ],
        compiler_params=pltpu.CompilerParams(collective_id=0, has_side_effects=True, vmem_limit_bytes=58 << 20),
        cost_estimate=pl.CostEstimate(flops=20_000_000_000, bytes_accessed=8_000_000, transcendentals=0),
        name="lead_gather",
    )(packed, base_tiles, w)


def finish_kernel(arr, base_ref, l_ref, m_ref, wb, o_ref):
    z = lax.axis_index("bit")
    f = lax.axis_index("front")
    j = pl.program_id(0)
    cols = []
    for col in range(6):
        v = base_ref[0, 0, 0, :, 128 * col:128 * col + 128]
        for g in range(2):
            v = v + spread(wb, g, lambda c, g=g: arr[g, 0, 0, :, 128 * c:128 * c + 128] + arr[g, 1, 0, :, 128 * c:128 * c + 128], col)
        cols.append(v)
    a = jnp.concatenate(cols, 1)
    for s in range(3):
        hi = 256 * s + 256
        o_ref[0, 0, 0, :, 256 * s:hi] = nt(a[:, :hi], m_ref[256 * s:hi, :hi])

    @pl.when((j == 0) & (f <= 2))
    def _():
        o_ref[0, 0, 0] = l_ref[pl.ds(pl.multiple_of((2 * f + z) * 128, 128), 128), :]


def finish(arrived, base_tiles, low, inv, wb):
    arr = arrived.reshape(2, 2, 8, 128, 512)
    full = pl.BlockSpec((768, 768), lambda j: (0, 0))
    return pl.pallas_call(
        finish_kernel,
        out_shape=jax.ShapeDtypeStruct((1, 1, 8, 128, 768), jnp.float32),
        grid=(8,),
        in_specs=[
            pl.BlockSpec((2, 2, 1, 128, 512), lambda j: (0, 0, j, 0, 0)),
            pl.BlockSpec((1, 1, 1, 128, 768), lambda j: (0, 0, j, 0, 0)),
            full,
            full,
            pl.BlockSpec((2, 8, 128), lambda j: (0, 0, 0)),
        ],
        out_specs=pl.BlockSpec((1, 1, 1, 128, 768), lambda j: (0, 0, j, 0, 0)),
        compiler_params=pltpu.CompilerParams(vmem_limit_bytes=40 << 20),
        name="finish_rows",
    )(arr, base_tiles, low, inv, wb)


def body(child_block, child_rows, child_cols, parent_base):
    f = lax.axis_index("front")
    dest = jnp.arange(32, dtype=jnp.int32)
    target = 32 * (f % 8) + 2 * (dest % 16) + dest // 16
    number = jnp.arange(1, 15, dtype=jnp.int32)
    pick = jnp.sum(jnp.where(child_rows[0, 0][None, :] == target[:, None], number[None, :], 0), axis=1)
    packed = pack(pick, child_block[0, 0])
    c1, c2 = child_cols[0, 1], child_cols[0, 2]
    masks = jnp.stack([c1 == 1, c1 == 2, c2 == 2, c1 == 3, c2 == 3, c2 == 4, c1 == 0, c1 == 0])
    w = jnp.broadcast_to(masks.astype(jnp.float32)[:, None], (8, 128))
    arrived = lax.all_to_all(packed, ("bit", "front"), split_axis=0, concat_axis=0, tiled=True)
    top, wb = lead(packed, parent_base, w)
    low, inv = chol(top.reshape(768, 768))
    return finish(arrived, parent_base, low, inv, wb)


def solution(mesh):
    mesh = Mesh(mesh.devices.reshape(4, 2, 16), ("pair", "bit", "front"))
    cube = ("pair", "bit")
    placed = (P(cube, "front"), P(cube, "front"), P(cube), P(cube, "front"))
    return jax.shard_map(body, mesh=mesh, in_specs=placed, out_specs=P(cube, "front"), check_vma=False)
```

```python
import jax
import jax.numpy as jnp
from jax import lax
from jax.experimental import pallas as pl
from jax.experimental.pallas import tpu as pltpu
from jax.sharding import Mesh
from jax.sharding import PartitionSpec as P

MESH = pl.DeviceIdType.MESH
HI = lax.Precision.HIGHEST
VM = pl.BlockSpec(memory_space=pltpu.VMEM)
ANY = pl.BlockSpec(memory_space=pl.ANY)


def nt(a,b,prec=HI):
    return lax.dot_general(a,b,(((1,),(1,)),((),())),precision=prec,preferred_element_type=jnp.float32)
def nn(a,b,prec=HI):
    return lax.dot_general(a,b,(((1,),(0,)),((),())),precision=prec,preferred_element_type=jnp.float32)
def base(block):
    S=block
    T=jnp.where(lax.broadcasted_iota(jnp.int32,(128,128),0)==lax.broadcasted_iota(jnp.int32,(128,128),1),1.0,0.0).astype(jnp.float32)
    U=[];M=[]
    for s in range(16):
        ur=[];mr=[]
        n=128-8*s
        subn=lax.broadcasted_iota(jnp.int32,(n,1),0)
        for r in range(0,8,2):
            i=8*s+r
            c0=S[:,i:i+1]; c1=S[:,i+1:i+2]
            a=c0[r:r+1]; b=c0[r+1:r+2]; c=c1[r+1:r+2]
            w0=S[r:r+1]; w1=S[r+1:r+2]; t0=T[r:r+1]; t1=T[r+1:r+2]
            rd=1.0/(a*c-b*b)
            keep=subn>r+1
            k0=jnp.where(keep,c0,0.0); k1=jnp.where(keep,c1,0.0)
            e0=k0*(c*rd)-k1*(b*rd); e1=k1*(a*rd)-k0*(b*rd)
            S=S-(e0*w0+e1*w1)
            T=T-(e0*t0+e1*t1)
            ra=lax.rsqrt(a); q=b*(ra*ra); rs=lax.rsqrt(c-b*q)
            ur+=[w0*ra,(w1-q*w0)*rs]; mr+=[t0*ra,(t1-q*t0)*rs]
        U.append(jnp.concatenate(ur,0)); M.append(jnp.concatenate(mr,0))
        if s<15: S=S[8:]; T=T[8:]
    return jnp.concatenate(U,0), jnp.concatenate(M,0)
NB=6
def chol_kernel(a_ref, l_ref, m_ref, w_ref):
    def blk(i,j): return (pl.ds(128*i,128),pl.ds(128*j,128))
    for i in range(NB):
        for j in range(i+1):
            v=a_ref[blk(i,j)]
            if i//2==j//2:
                v=0.5*(v+(v.T if i==j else a_ref[blk(j,i)].T))
            w_ref[blk(i,j)]=v
    tri=lax.broadcasted_iota(jnp.int32,(128,128),0)>=lax.broadcasted_iota(jnp.int32,(128,128),1)
    zero=jnp.zeros((128,128),jnp.float32)
    for k in range(NB):
        U,M=base(w_ref[blk(k,k)])
        l_ref[blk(k,k)]=jnp.where(tri,U.T,0.0)
        m_ref[blk(k,k)]=M
        for j in range(k+1,NB):
            l_ref[blk(k,j)]=zero; m_ref[blk(k,j)]=zero
        if k+1<NB:
            n=128*(NB-1-k); r0=128*(k+1)
            P=nt(w_ref[pl.ds(r0,n),pl.ds(128*k,128)],M)
            l_ref[pl.ds(r0,n),pl.ds(128*k,128)]=P
            for j in range(k+1,NB):
                q0=128*(j-k-1)
                w_ref[pl.ds(128*j,n-q0),pl.ds(128*j,128)]-=nt(P[q0:],P[q0:q0+128])
        if k>0:
            acc=nn(l_ref[pl.ds(128*k,128),pl.ds(0,128*k)],m_ref[pl.ds(0,128*k),pl.ds(0,128*k)])
            m_ref[pl.ds(128*k,128),pl.ds(0,128*k)]=-nn(M,acc)
def order_offsets():
    rest = [(n // 16, (n // 4) % 4, (n // 2) % 2, n % 2) for n in range(1, 32)]
    total = (16, 16, 16, 16)
    load = [0, 0, 0, 0]
    out = []

    def use(o):
        dz, dy, dx, dk = o
        return (dz, dx, int(dy in (1, 2)), int(dy in (2, 3)))

    while rest:
        share = (len(out) + 1) / 31
        best = min(rest, key=lambda o: (sum((a + b - t * share) ** 2 for a, b, t in zip(load, use(o), total)), (o[0] * 7 + o[1] * 3 + o[2] * 5 + o[3] * 11) % 13))
        rest.remove(best)
        out.append(best)
        load = [a + b for a, b in zip(load, use(best))]
    return out


OFFSETS = order_offsets()
BATCH = (3, 3, 3, 3)


def spread(w, g, s, col):
    if col == 0:
        return s(0)
    if col == 5:
        return s(3)
    if col == 1:
        return s(1) * w[g, 0:1]
    if col == 2:
        return s(1) * w[g, 1:2] + s(2) * w[g, 2:3]
    if col == 3:
        return s(1) * w[g, 3:4] + s(2) * w[g, 4:5]
    return s(2) * w[g, 5:6]


def front_kernel(pick, child_hbm, base_hbm, w_in, out, child, packed, arr, base, lbuf, cbuf, wb, top, work, low, inv, inv_hi, inv_lo, res,
                 lsem, osem, ssem, rsem, dsem, wsem, csem, ysem, xsem, ksem):
    pair = lax.axis_index("pair")
    z = lax.axis_index("bit")
    f = lax.axis_index("front")
    y, x, k = f // 4, (f // 2) % 2, f % 2
    me = z * 16 + f

    def at(dz, dy, dx, dk):
        return (pair, (z + dz) % 2, ((y + dy) % 4) * 4 + ((x + dx) % 2) * 2 + (k + dk) % 2)

    child_copy = pltpu.make_async_copy(child_hbm, child, lsem.at[0])
    base_copy = pltpu.make_async_copy(base_hbm.at[0, 0], base, lsem.at[1])
    child_copy.start()
    base_copy.start()
    bar = pltpu.get_barrier_semaphore()
    for n in range(1, 32):
        pl.semaphore_signal(bar, inc=1, device_id=at(n // 16, (n // 4) % 4, (n // 2) % 2, n % 2), device_id_type=MESH)
    pl.semaphore_wait(bar, 31)

    wb[z] = w_in[...]
    wcopy = pltpu.make_async_remote_copy(
        src_ref=w_in, dst_ref=wb.at[z], send_sem=wsem.at[0], recv_sem=wsem.at[1],
        device_id=at(1, 0, 0, 0), device_id_type=MESH)
    wcopy.start()
    child_copy.wait()

    def tile_for(d):
        i = pick[d]
        return jnp.where(i > 0, child[jnp.maximum(i - 1, 0)], 0.0)

    source = (f == 0) | (f == 8)
    half = z * 2 + y // 2
    widths = (256, 384, 512)

    def child_send(b, q):
        n = widths[q]
        return pltpu.make_async_remote_copy(
            src_ref=lbuf.at[3 * b + q, :, pl.ds(0, n)], dst_ref=cbuf.at[half, :, pl.ds(0, n)], send_sem=dsem.at[b * 3 + q],
            recv_sem=csem.at[half], device_id=(pair, b, q), device_id_type=MESH)

    def own(b, q):
        return (f == q) & (z == b)

    @pl.when(source)
    def _():
        for q in (2, 1, 0):
            for b in range(2):
                lbuf[3 * b + q] = tile_for(16 * b + q)

                @pl.when(jnp.logical_not(own(b, q)))
                def _(b=b, q=q):
                    child_send(b, q).start()

    def offset(n):
        a, b = OFFSETS[n], OFFSETS[30 - n]
        return tuple(u + k * (v - u) for u, v in zip(a, b))

    def bulk(n):
        dz, dy, dx, dk = offset(n)
        to = at(dz, dy, dx, dk)
        return to, pltpu.make_async_remote_copy(
            src_ref=packed.at[n], dst_ref=arr.at[me], send_sem=ssem.at[n], recv_sem=rsem.at[me], device_id=to, device_id_type=MESH)

    def batch(lo, hi):
        for n in range(lo, hi):
            to, copy = bulk(n)
            packed[n] = tile_for(to[1] * 16 + to[2])
            copy.start()

    marks = [sum(BATCH[:i]) for i in range(5)]
    batch(0, marks[1])
    arr[me] = tile_for(me)
    base_copy.wait()
    wcopy.wait_recv()

    for q in range(3):
        n = widths[q]

        @pl.when(f == q)
        def _(q=q, n=n):
            for s in range(4):
                mine_too = (f == 0) & (half == s)

                @pl.when(jnp.logical_not(mine_too))
                def _(s=s):
                    pltpu.make_async_remote_copy(
                        src_ref=lbuf.at[0, :, pl.ds(0, n)], dst_ref=cbuf.at[s, :, pl.ds(0, n)], send_sem=dsem.at[0],
                        recv_sem=csem.at[s], device_id=at(1, 0, 0, 0), device_id_type=MESH).wait_recv()

                if q == 0:
                    @pl.when(mine_too)
                    def _(s=s):
                        cbuf[s, :, 0:256] = lbuf[3 * z, :, 0:256]
            row = pl.ds(pl.multiple_of((2 * q + z) * 128, 128), 128)
            for col in range(2 * q + 2):
                v = base[0, :, 128 * col:128 * col + 128]
                for g in range(2):
                    v = v + spread(wb, g, lambda c, g=g: cbuf[2 * g, :, 128 * c:128 * c + 128] + cbuf[2 * g + 1, :, 128 * c:128 * c + 128], col)
                top[row, 128 * col:128 * col + 128] = v

    def tile_copy(q, zz, send, recv, to):
        piece = top.at[pl.ds(pl.multiple_of((2 * q + zz) * 128, 128), 128), pl.ds(0, 256 * q + 256)]
        return pltpu.make_async_remote_copy(
            src_ref=piece, dst_ref=piece, send_sem=send, recv_sem=recv, device_id=to, device_id_type=MESH)

    mine = f % 4
    for q in range(3):
        @pl.when(f == q)
        def _(q=q):
            for n, dy in enumerate((2, 1, 3)):
                tile_copy(q, z, dsem.at[6 + n], ysem.at[0], at(0, dy, 0, 0)).start()
    batch(marks[1], marks[2])
    for q in range(3):
        @pl.when(mine == q)
        def _(q=q):
            @pl.when(y > 0)
            def _():
                tile_copy(q, z, dsem.at[6], ysem.at[0], at(0, 1, 0, 0)).wait_recv()

            for n, (dz, dx) in enumerate(((1, 1), (0, 1), (1, 0))):
                tile_copy(q, z, dsem.at[9 + n], xsem.at[2 * q + z], at(dz, 0, dx, 0)).start()
            tile_copy(q, z, dsem.at[(14 if q == 2 else 12) + z], ksem.at[2 * q + z], at(0, 0, 0, 1)).start()
    batch(marks[2], marks[3])
    for q in range(3):
        @pl.when(k == q % 2)
        def _(q=q):
            for zz in range(2):
                @pl.when((mine != q) | (z != zz))
                def _(zz=zz):
                    tile_copy(q, zz, dsem.at[9], xsem.at[2 * q + zz], at(0, 0, 1, 0)).wait_recv()
                    tile_copy(q, zz, dsem.at[(14 if q == 2 else 12) + zz], ksem.at[2 * q + zz], at(0, 0, 0, 1)).start()
    batch(marks[3], marks[4])
    for q in range(3):
        @pl.when(k != q % 2)
        def _(q=q):
            for zz in range(2):
                tile_copy(q, zz, dsem.at[9], ksem.at[2 * q + zz], at(0, 0, 0, 1)).wait_recv()
    batch(marks[4], 31)

    chol_kernel(top, low, inv, work)
    v = inv[...]
    hi = v.astype(jnp.bfloat16)
    inv_hi[...] = hi
    inv_lo[...] = (v - hi.astype(jnp.float32)).astype(jnp.bfloat16)

    def slot_of(e):
        return ((y + e // 4) % 2) * 4 + ((x + e // 2) % 2) * 2 + (k + e) % 2

    def out_copy(e):
        j = slot_of(e)
        return pltpu.make_async_copy(res.at[e // 2, pl.ds(128 * (e % 2), 128)], out.at[0, 0, j], osem.at[e])

    for step in range(4):
        rows = []
        for e in (2 * step, 2 * step + 1):
            j = slot_of(e)
            for g in range(2):
                for h in range(2):
                    src = g * 16 + h * 8 + j

                    @pl.when(src != me)
                    def _(src=src):
                        pltpu.make_async_remote_copy(
                            src_ref=packed.at[0], dst_ref=arr.at[src], send_sem=ssem.at[0], recv_sem=rsem.at[src],
                            device_id=at(1, 0, 0, 0), device_id_type=MESH).wait_recv()
            cols = []
            for col in range(6):
                v = base[j, :, 128 * col:128 * col + 128]
                for g in range(2):
                    v = v + spread(wb, g, lambda c, g=g: arr[g * 16 + j, :, 128 * c:128 * c + 128] + arr[g * 16 + 8 + j, :, 128 * c:128 * c + 128], col)
                cols.append(v)
            rows.append(jnp.concatenate(cols, 1))
        a = jnp.concatenate(rows, 0)
        a_hi = a.astype(jnp.bfloat16)
        a_lo = (a - a_hi.astype(jnp.float32)).astype(jnp.bfloat16)
        for s in range(3):
            n = 256 * s + 256
            m_hi, m_lo = inv_hi[n - 256:n, :n], inv_lo[n - 256:n, :n]
            res[step, :, n - 256:n] = (nt(a_lo[:, :n], m_hi, None) + nt(a_hi[:, :n], m_lo, None)) + nt(a_hi[:, :n], m_hi, None)
        for e in (2 * step, 2 * step + 1):
            @pl.when((slot_of(e) == 0) & (f <= 2))
            def _(e=e):
                res[step, 128 * (e % 2):128 * (e % 2) + 128, :] = low[pl.ds(pl.multiple_of((2 * f + z) * 128, 128), 128), :]

            out_copy(e).start()

    for n in range(31):
        bulk(n)[1].wait_send()
    wcopy.wait_send()

    @pl.when(source)
    def _():
        for q in range(3):
            for b in range(2):
                @pl.when(jnp.logical_not(own(b, q)))
                def _(b=b, q=q):
                    child_send(b, q).wait_send()

    for q in range(3):
        @pl.when(f == q)
        def _(q=q):
            for n in range(3):
                tile_copy(q, z, dsem.at[6 + n], ysem.at[0], at(0, 1, 0, 0)).wait_send()

        @pl.when(mine == q)
        def _(q=q):
            for n in range(3):
                tile_copy(q, z, dsem.at[9 + n], xsem.at[2 * q + z], at(0, 0, 1, 0)).wait_send()

        @pl.when(k == q % 2)
        def _(q=q):
            for zz in range(2):
                tile_copy(q, zz, dsem.at[(14 if q == 2 else 12) + zz], ksem.at[2 * q + zz], at(0, 0, 0, 1)).wait_send()
    for e in range(8):
        out_copy(e).wait()


def fronts(pick, tiles, base_tiles, w):
    f32 = jnp.float32
    square = pltpu.VMEM((768, 768), f32)
    dma = pltpu.SemaphoreType.DMA
    return pl.pallas_call(
        front_kernel,
        out_shape=jax.ShapeDtypeStruct((1, 1, 8, 128, 768), f32),
        in_specs=[pl.BlockSpec(memory_space=pltpu.SMEM), ANY, ANY, VM],
        out_specs=ANY,
        scratch_shapes=[
            pltpu.VMEM((14, 128, 512), f32),
            pltpu.VMEM((31, 128, 512), f32),
            pltpu.VMEM((32, 128, 512), f32),
            pltpu.VMEM((8, 128, 768), f32),
            pltpu.VMEM((6, 128, 512), f32),
            pltpu.VMEM((4, 128, 512), f32),
            pltpu.VMEM((2, 8, 128), f32),
            square, square, square, square,
            pltpu.VMEM((768, 768), jnp.bfloat16),
            pltpu.VMEM((768, 768), jnp.bfloat16),
            pltpu.VMEM((4, 256, 768), f32),
            dma((2,)), dma((8,)), dma((31,)), dma((32,)), dma((16,)), dma((2,)), dma((4,)), dma((1,)), dma((6,)), dma((6,)),
        ],
        compiler_params=pltpu.CompilerParams(collective_id=0, has_side_effects=True, vmem_limit_bytes=58 << 20),
        name="fronts",
    )(pick, tiles, base_tiles, w)


def body(child_block, child_rows, child_cols, parent_base):
    f = lax.axis_index("front")
    dest = jnp.arange(32, dtype=jnp.int32)
    target = 32 * (f % 8) + 2 * (dest % 16) + dest // 16
    number = jnp.arange(1, 15, dtype=jnp.int32)
    pick = jnp.sum(jnp.where(child_rows[0, 0][None, :] == target[:, None], number[None, :], 0), axis=1)
    c1, c2 = child_cols[0, 1], child_cols[0, 2]
    masks = jnp.stack([c1 == 1, c1 == 2, c2 == 2, c1 == 3, c2 == 3, c2 == 4, c1 == 0, c1 == 0])
    w = jnp.broadcast_to(masks.astype(jnp.float32)[:, None], (8, 128))
    return fronts(pick, child_block[0, 0], parent_base, w)


def solution(mesh):
    mesh = Mesh(mesh.devices.reshape(4, 2, 16), ("pair", "bit", "front"))
    cube = ("pair", "bit")
    placed = (P(cube, "front"), P(cube, "front"), P(cube), P(cube, "front"))
    return jax.shard_map(body, mesh=mesh, in_specs=placed, out_specs=P(cube, "front"), check_vma=False)
```

```python
import jax
import jax.numpy as jnp
from jax import lax
from jax.experimental import pallas as pl
from jax.experimental.pallas import tpu as pltpu
from jax.sharding import Mesh
from jax.sharding import PartitionSpec as P

MESH = pl.DeviceIdType.MESH
HI = lax.Precision.HIGHEST
VM = pl.BlockSpec(memory_space=pltpu.VMEM)
ANY = pl.BlockSpec(memory_space=pl.ANY)
SM = pl.BlockSpec(memory_space=pltpu.SMEM)


def nt(a,b,prec=HI):
    return lax.dot_general(a,b,(((1,),(1,)),((),())),precision=prec,preferred_element_type=jnp.float32)
def nn(a,b,prec=HI):
    return lax.dot_general(a,b,(((1,),(0,)),((),())),precision=prec,preferred_element_type=jnp.float32)
def full(x): return jnp.broadcast_to(x,(8,128))
def base(block):
    sub=lax.broadcasted_iota(jnp.int32,(8,128),0)
    S=block
    T=jnp.where(lax.broadcasted_iota(jnp.int32,(128,128),0)==lax.broadcasted_iota(jnp.int32,(128,128),1),1.0,0.0).astype(jnp.float32)
    U=[];M=[]
    for s in range(16):
        n=128-8*s
        R=S[:8]; Q=T[:8]
        C=[full(R[:,8*s+j:8*s+j+1]) for j in range(8)]
        D={(i,j):full(C[j][i:i+1]) for i in range(8) for j in range(i,8)}
        ra=[None]*8; E={}
        for p in range(0,8,2):
            a,b,c=D[p,p],D[p,p+1],D[p+1,p+1]
            rs=lax.rsqrt(a*c-b*b); rd=rs*rs
            A,B,Cc=c*rd,b*rd,a*rd
            r0=lax.rsqrt(a); ra[p]=r0; ra[p+1]=(a*r0)*rs; E[p+1,p]=b*(r0*r0)
            for i in range(p+2,8):
                x0,x1=D[p,i],D[p+1,i]
                e0=x0*A-x1*B; e1=x1*Cc-x0*B
                E[i,p]=e0; E[i,p+1]=e1
                for j in range(i,8):
                    D[i,j]=D[i,j]-(e0*D[p,j]+e1*D[p+1,j])
        W=[full(R[i:i+1]) for i in range(8)]; V=[full(Q[i:i+1]) for i in range(8)]
        for p in range(0,8,2):
            for i in range(p+2,8):
                W[i]=W[i]-(E[i,p]*W[p]+E[i,p+1]*W[p+1]); V[i]=V[i]-(E[i,p]*V[p]+E[i,p+1]*V[p+1])
        for p in range(0,8,2):
            W[p+1]=W[p+1]-E[p+1,p]*W[p]; V[p+1]=V[p+1]-E[p+1,p]*V[p]
        W=[w*r for w,r in zip(W,ra)]; V=[v*r for v,r in zip(V,ra)]
        def merge(rows):
            o=rows[7]
            for k in range(7): o=jnp.where(sub==k,rows[k],o)
            return o
        U.append(merge(W)); M.append(merge(V))
        if s<15:
            S=S[8:]; T=T[8:]
            rows=[]; trows=[]
            for t in range((n-8)//8):
                St=S[8*t:8*t+8]; Tt=T[8*t:8*t+8]
                Z=[full(St[:,8*s+j:8*s+j+1]) for j in range(8)]
                for p in range(0,8,2):
                    for i in range(p+2,8):
                        Z[i]=Z[i]-(E[i,p]*Z[p]+E[i,p+1]*Z[p+1])
                for p in range(0,8,2):
                    Z[p+1]=Z[p+1]-E[p+1,p]*Z[p]
                Z=[z*r for z,r in zip(Z,ra)]
                def dot8(X):
                    m=[z*x for z,x in zip(Z,X)]
                    return ((m[0]+m[1])+(m[2]+m[3]))+((m[4]+m[5])+(m[6]+m[7]))
                rows.append(St-dot8(W)); trows.append(Tt-dot8(V))
            S=jnp.concatenate(rows,0); T=jnp.concatenate(trows,0)
    return jnp.concatenate(U,0), jnp.concatenate(M,0)

def chol_kernel(a_ref, l_ref, m_ref, w_ref, d_ref):
    def blk(i, j):
        return (pl.ds(128 * i, 128), pl.ds(128 * j, 128))

    zero = jnp.zeros((128, 128), jnp.float32)
    for i in range(6):
        for j in range(6):
            if j > i:
                l_ref[blk(i, j)] = zero
                m_ref[blk(i, j)] = zero
                continue
            v = a_ref[blk(i, j)]
            if i // 2 == j // 2:
                v = 0.5 * (v + (v.T if i == j else a_ref[blk(j, i)].T))
            w_ref[blk(i, j)] = v
    tri = lax.broadcasted_iota(jnp.int32, (128, 128), 0) >= lax.broadcasted_iota(jnp.int32, (128, 128), 1)

    def step(k, carry):
        at = pl.multiple_of(k * 128, 128)
        here = (pl.ds(at, 128), pl.ds(at, 128))
        U, M = base(w_ref[here])
        l_ref[here] = jnp.where(tri, U.T, 0.0)
        m_ref[here] = M
        d_ref[...] = M
        for kk in range(6):
            @pl.when(k == kk)
            def _(kk=kk):
                M = d_ref[...]
                if kk < 5:
                    n, r0 = 128 * (5 - kk), 128 * (kk + 1)
                    P = nt(w_ref[pl.ds(r0, n), pl.ds(128 * kk, 128)], M)
                    l_ref[pl.ds(r0, n), pl.ds(128 * kk, 128)] = P
                    for j in range(kk + 1, 6):
                        q0 = 128 * (j - kk - 1)
                        w_ref[pl.ds(128 * j, n - q0), pl.ds(128 * j, 128)] -= nt(P[q0:], P[q0:q0 + 128])
                if kk > 0:
                    acc = nn(l_ref[pl.ds(128 * kk, 128), pl.ds(0, 128 * kk)], m_ref[pl.ds(0, 128 * kk), pl.ds(0, 128 * kk)])
                    m_ref[pl.ds(128 * kk, 128), pl.ds(0, 128 * kk)] = -nn(M, acc)
        return carry

    lax.fori_loop(0, 6, step, 0)


def order_offsets():
    rest = [(n // 16, (n // 4) % 4, (n // 2) % 2, n % 2) for n in range(1, 32)]
    total = (16, 16, 16, 16)
    load = [0, 0, 0, 0]
    out = []

    def use(o):
        dz, dy, dx, dk = o
        return (dz, dx, int(dy in (1, 2)), int(dy in (2, 3)))

    while rest:
        share = (len(out) + 1) / 31
        best = min(rest, key=lambda o: (sum((a + b - t * share) ** 2 for a, b, t in zip(load, use(o), total)), (o[0] * 7 + o[1] * 3 + o[2] * 5 + o[3] * 11) % 13))
        rest.remove(best)
        out.append(best)
        load = [a + b for a, b in zip(load, use(best))]
    return out


OFFSETS = order_offsets()
BATCH = (8, 3, 3, 3)


def spread(w, g, s, col):
    if col == 0:
        return s(0)
    if col == 5:
        return s(3)
    if col == 1:
        return s(1) * w[g, 0:1]
    if col == 2:
        return s(1) * w[g, 1:2] + s(2) * w[g, 2:3]
    if col == 3:
        return s(1) * w[g, 3:4] + s(2) * w[g, 4:5]
    return s(2) * w[g, 5:6]


def front_kernel(rows_ref, cols_ref, child_hbm, base_hbm, res, child, packed, arr, base, lbuf, cbuf, w_in, wb, top, work, low, inv, diag, inv_hi, inv_lo,
                 lsem, ssem, rsem, dsem, wsem, csem, ysem, xsem, ksem):
    pair = lax.axis_index("pair")
    z = lax.axis_index("bit")
    f = lax.axis_index("front")
    y, x, k = f // 4, (f // 2) % 2, f % 2
    me = z * 16 + f

    def at(dz, dy, dx, dk):
        return (pair, (z + dz) % 2, ((y + dy) % 4) * 4 + ((x + dx) % 2) * 2 + (k + dk) % 2)

    child_copy = pltpu.make_async_copy(child_hbm, child, lsem.at[0])
    base_copy = pltpu.make_async_copy(base_hbm.at[0, 0], base, lsem.at[1])
    child_copy.start()
    base_copy.start()
    bar = pltpu.get_barrier_semaphore()
    for n in range(1, 32):
        pl.semaphore_signal(bar, inc=1, device_id=at(n // 16, (n // 4) % 4, (n // 2) % 2, n % 2), device_id_type=MESH)
    pl.semaphore_wait(bar, 31)

    c1, c2 = cols_ref[0, 1], cols_ref[0, 2]
    lines = [jnp.broadcast_to(jnp.where(c, 1.0, 0.0), (1, 128)) for c in (c1 == 1, c1 == 2, c2 == 2, c1 == 3, c2 == 3, c2 == 4)]
    masks = jnp.concatenate(lines + [jnp.zeros((2, 128), jnp.float32)], 0)
    w_in[...] = masks
    wb[z] = masks
    wcopy = pltpu.make_async_remote_copy(
        src_ref=w_in, dst_ref=wb.at[z], send_sem=wsem.at[0], recv_sem=wsem.at[1],
        device_id=at(1, 0, 0, 0), device_id_type=MESH)
    wcopy.start()
    child_copy.wait()

    def tile_for(d):
        target = 32 * (f % 8) + 2 * (d % 16) + d // 16
        i = jnp.int32(0)
        for t in range(14):
            i = jnp.where(rows_ref[t] == target, t + 1, i)
        return jnp.where(i > 0, child[jnp.maximum(i - 1, 0)], 0.0)

    source = (f == 0) | (f == 8)
    half = z * 2 + y // 2
    widths = (256, 384, 512)

    def child_send(b, q):
        n = widths[q]
        return pltpu.make_async_remote_copy(
            src_ref=lbuf.at[3 * b + q, :, pl.ds(0, n)], dst_ref=cbuf.at[half, :, pl.ds(0, n)], send_sem=dsem.at[b * 3 + q],
            recv_sem=csem.at[half], device_id=(pair, b, q), device_id_type=MESH)

    def own(b, q):
        return (f == q) & (z == b)

    @pl.when(source)
    def _():
        for q in (2, 1, 0):
            for b in range(2):
                lbuf[3 * b + q] = tile_for(16 * b + q)

                @pl.when(jnp.logical_not(own(b, q)))
                def _(b=b, q=q):
                    child_send(b, q).start()

    def offset(n):
        a, b = OFFSETS[n], OFFSETS[30 - n]
        return tuple(u + k * (v - u) for u, v in zip(a, b))

    def bulk(n):
        dz, dy, dx, dk = offset(n)
        to = at(dz, dy, dx, dk)
        return to, pltpu.make_async_remote_copy(
            src_ref=packed.at[n], dst_ref=arr.at[me], send_sem=ssem.at[n], recv_sem=rsem.at[me], device_id=to, device_id_type=MESH)

    def batch(lo, hi):
        for n in range(lo, hi):
            to, copy = bulk(n)
            packed[n] = tile_for(to[1] * 16 + to[2])
            copy.start()

    marks = [sum(BATCH[:i]) for i in range(5)]
    batch(0, marks[1])
    arr[me] = tile_for(me)
    base_copy.wait()
    wcopy.wait_recv()

    for q in range(3):
        n = widths[q]

        @pl.when(f == q)
        def _(q=q, n=n):
            for s in range(4):
                mine_too = (f == 0) & (half == s)

                @pl.when(jnp.logical_not(mine_too))
                def _(s=s):
                    pltpu.make_async_remote_copy(
                        src_ref=lbuf.at[0, :, pl.ds(0, n)], dst_ref=cbuf.at[s, :, pl.ds(0, n)], send_sem=dsem.at[0],
                        recv_sem=csem.at[s], device_id=at(1, 0, 0, 0), device_id_type=MESH).wait_recv()

                if q == 0:
                    @pl.when(mine_too)
                    def _(s=s):
                        cbuf[s, :, 0:256] = lbuf[3 * z, :, 0:256]
            row = pl.ds(pl.multiple_of((2 * q + z) * 128, 128), 128)
            for col in range(2 * q + 2):
                v = base[0, :, 128 * col:128 * col + 128]
                for g in range(2):
                    v = v + spread(wb, g, lambda c, g=g: cbuf[2 * g, :, 128 * c:128 * c + 128] + cbuf[2 * g + 1, :, 128 * c:128 * c + 128], col)
                top[row, 128 * col:128 * col + 128] = v

    def tile_copy(q, zz, send, recv, to):
        piece = top.at[pl.ds(pl.multiple_of((2 * q + zz) * 128, 128), 128), pl.ds(0, 256 * q + 256)]
        return pltpu.make_async_remote_copy(
            src_ref=piece, dst_ref=piece, send_sem=send, recv_sem=recv, device_id=to, device_id_type=MESH)

    mine = f % 4
    for q in range(3):
        @pl.when(f == q)
        def _(q=q):
            for n, dy in enumerate((2, 1, 3)):
                tile_copy(q, z, dsem.at[6 + n], ysem.at[0], at(0, dy, 0, 0)).start()
    batch(marks[1], marks[2])
    for q in range(3):
        @pl.when(mine == q)
        def _(q=q):
            @pl.when(y > 0)
            def _():
                tile_copy(q, z, dsem.at[6], ysem.at[0], at(0, 1, 0, 0)).wait_recv()

            for n, (dz, dx) in enumerate(((1, 1), (0, 1), (1, 0))):
                tile_copy(q, z, dsem.at[9 + n], xsem.at[2 * q + z], at(dz, 0, dx, 0)).start()
            tile_copy(q, z, dsem.at[(14 if q == 2 else 12) + z], ksem.at[2 * q + z], at(0, 0, 0, 1)).start()
    batch(marks[2], marks[3])
    for q in range(3):
        @pl.when(k == q % 2)
        def _(q=q):
            for zz in range(2):
                @pl.when((mine != q) | (z != zz))
                def _(zz=zz):
                    tile_copy(q, zz, dsem.at[9], xsem.at[2 * q + zz], at(0, 0, 1, 0)).wait_recv()
                    tile_copy(q, zz, dsem.at[(14 if q == 2 else 12) + zz], ksem.at[2 * q + zz], at(0, 0, 0, 1)).start()
    batch(marks[3], marks[4])
    for q in range(3):
        @pl.when(k != q % 2)
        def _(q=q):
            for zz in range(2):
                tile_copy(q, zz, dsem.at[9], ksem.at[2 * q + zz], at(0, 0, 0, 1)).wait_recv()
    batch(marks[4], 31)

    chol_kernel(top, low, inv, work, diag)
    v = inv[...]
    hi = v.astype(jnp.bfloat16)
    inv_hi[...] = hi
    inv_lo[...] = (v - hi.astype(jnp.float32)).astype(jnp.bfloat16)

    def slot_of(e):
        return ((y + e // 4) % 2) * 4 + ((x + e // 2) % 2) * 2 + (k + e) % 2

    for step in range(4):
        rows = []
        for e in (2 * step, 2 * step + 1):
            j = slot_of(e)
            for g in range(2):
                for h in range(2):
                    src = g * 16 + h * 8 + j

                    @pl.when(src != me)
                    def _(src=src):
                        pltpu.make_async_remote_copy(
                            src_ref=packed.at[0], dst_ref=arr.at[src], send_sem=ssem.at[0], recv_sem=rsem.at[src],
                            device_id=at(1, 0, 0, 0), device_id_type=MESH).wait_recv()
            cols = []
            for col in range(6):
                v = base[j, :, 128 * col:128 * col + 128]
                for g in range(2):
                    v = v + spread(wb, g, lambda c, g=g: arr[g * 16 + j, :, 128 * c:128 * c + 128] + arr[g * 16 + 8 + j, :, 128 * c:128 * c + 128], col)
                cols.append(v)
            rows.append(jnp.concatenate(cols, 1))
        a = jnp.concatenate(rows, 0)
        a_hi = a.astype(jnp.bfloat16)
        a_lo = (a - a_hi.astype(jnp.float32)).astype(jnp.bfloat16)
        for s in range(3):
            n = 256 * s + 256
            m_hi, m_lo = inv_hi[n - 256:n, :n], inv_lo[n - 256:n, :n]
            v = (nt(a_lo[:, :n], m_hi, None) + nt(a_hi[:, :n], m_lo, None)) + nt(a_hi[:, :n], m_hi, None)
            for e in (0, 1):
                res[0, 0, slot_of(2 * step + e), :, n - 256:n] = v[128 * e:128 * e + 128]
        for e in (2 * step, 2 * step + 1):
            @pl.when((slot_of(e) == 0) & (f <= 2))
            def _(e=e):
                res[0, 0, 0] = low[pl.ds(pl.multiple_of((2 * f + z) * 128, 128), 128), :]

    for n in range(31):
        bulk(n)[1].wait_send()
    wcopy.wait_send()

    @pl.when(source)
    def _():
        for q in range(3):
            for b in range(2):
                @pl.when(jnp.logical_not(own(b, q)))
                def _(b=b, q=q):
                    child_send(b, q).wait_send()

    for q in range(3):
        @pl.when(f == q)
        def _(q=q):
            for n in range(3):
                tile_copy(q, z, dsem.at[6 + n], ysem.at[0], at(0, 1, 0, 0)).wait_send()

        @pl.when(mine == q)
        def _(q=q):
            for n in range(3):
                tile_copy(q, z, dsem.at[9 + n], xsem.at[2 * q + z], at(0, 0, 1, 0)).wait_send()

        @pl.when(k == q % 2)
        def _(q=q):
            for zz in range(2):
                tile_copy(q, zz, dsem.at[(14 if q == 2 else 12) + zz], ksem.at[2 * q + zz], at(0, 0, 0, 1)).wait_send()


def fronts(rows, cols, tiles, base_tiles):
    f32 = jnp.float32
    square = pltpu.VMEM((768, 768), f32)
    dma = pltpu.SemaphoreType.DMA
    return pl.pallas_call(
        front_kernel,
        out_shape=jax.ShapeDtypeStruct((1, 1, 8, 128, 768), f32),
        in_specs=[SM, SM, ANY, ANY],
        out_specs=VM,
        scratch_shapes=[
            pltpu.VMEM((14, 128, 512), f32),
            pltpu.VMEM((31, 128, 512), f32),
            pltpu.VMEM((32, 128, 512), f32),
            pltpu.VMEM((8, 128, 768), f32),
            pltpu.VMEM((6, 128, 512), f32),
            pltpu.VMEM((4, 128, 512), f32),
            pltpu.VMEM((8, 128), f32),
            pltpu.VMEM((2, 8, 128), f32),
            square, square, square, square,
            pltpu.VMEM((128, 128), f32),
            pltpu.VMEM((768, 768), jnp.bfloat16),
            pltpu.VMEM((768, 768), jnp.bfloat16),
            dma((2,)), dma((31,)), dma((32,)), dma((16,)), dma((2,)), dma((4,)), dma((1,)), dma((6,)), dma((6,)),
        ],
        compiler_params=pltpu.CompilerParams(collective_id=0, has_side_effects=True, vmem_limit_bytes=46 << 20),
        name="fronts",
    )(rows, cols, tiles, base_tiles)


def body(child_block, child_rows, child_cols, parent_base):
    return fronts(child_rows[0, 0], child_cols, child_block[0, 0], parent_base)


def solution(mesh):
    mesh = Mesh(mesh.devices.reshape(4, 2, 16), ("pair", "bit", "front"))
    cube = ("pair", "bit")
    placed = (P(cube, "front"), P(cube, "front"), P(cube), P(cube, "front"))
    return jax.shard_map(body, mesh=mesh, in_specs=placed, out_specs=P(cube, "front"), check_vma=False)
```

```python
import jax
import jax.numpy as jnp
from jax import lax
from jax.experimental import pallas as pl
from jax.experimental.pallas import tpu as pltpu
from jax.sharding import Mesh
from jax.sharding import PartitionSpec as P

MESH = pl.DeviceIdType.MESH
HI = lax.Precision.HIGHEST
VM = pl.BlockSpec(memory_space=pltpu.VMEM)
ANY = pl.BlockSpec(memory_space=pl.ANY)
SM = pl.BlockSpec(memory_space=pltpu.SMEM)


def nt(a,b,prec=HI):
    return lax.dot_general(a,b,(((1,),(1,)),((),())),precision=prec,preferred_element_type=jnp.float32)
def nn(a,b,prec=HI):
    return lax.dot_general(a,b,(((1,),(0,)),((),())),precision=prec,preferred_element_type=jnp.float32)
def full(x): return jnp.broadcast_to(x,(8,128))
def base(block):
    sub=lax.broadcasted_iota(jnp.int32,(8,128),0)
    S=block
    T=jnp.where(lax.broadcasted_iota(jnp.int32,(128,128),0)==lax.broadcasted_iota(jnp.int32,(128,128),1),1.0,0.0).astype(jnp.float32)
    U=[];M=[]
    for s in range(16):
        n=128-8*s
        R=S[:8]; Q=T[:8]
        C=[full(R[:,8*s+j:8*s+j+1]) for j in range(8)]
        D={(i,j):full(C[j][i:i+1]) for i in range(8) for j in range(i,8)}
        ra=[None]*8; E={}
        for p in range(0,8,2):
            a,b,c=D[p,p],D[p,p+1],D[p+1,p+1]
            rs=lax.rsqrt(a*c-b*b); rd=rs*rs
            A,B,Cc=c*rd,b*rd,a*rd
            r0=lax.rsqrt(a); ra[p]=r0; ra[p+1]=(a*r0)*rs; E[p+1,p]=b*(r0*r0)
            for i in range(p+2,8):
                x0,x1=D[p,i],D[p+1,i]
                e0=x0*A-x1*B; e1=x1*Cc-x0*B
                E[i,p]=e0; E[i,p+1]=e1
                for j in range(i,8):
                    D[i,j]=D[i,j]-(e0*D[p,j]+e1*D[p+1,j])
        W=[full(R[i:i+1]) for i in range(8)]; V=[full(Q[i:i+1]) for i in range(8)]
        for p in range(0,8,2):
            for i in range(p+2,8):
                W[i]=W[i]-(E[i,p]*W[p]+E[i,p+1]*W[p+1]); V[i]=V[i]-(E[i,p]*V[p]+E[i,p+1]*V[p+1])
        for p in range(0,8,2):
            W[p+1]=W[p+1]-E[p+1,p]*W[p]; V[p+1]=V[p+1]-E[p+1,p]*V[p]
        W=[w*r for w,r in zip(W,ra)]; V=[v*r for v,r in zip(V,ra)]
        def merge(rows):
            o=rows[7]
            for k in range(7): o=jnp.where(sub==k,rows[k],o)
            return o
        U.append(merge(W)); M.append(merge(V))
        if s<15:
            S=S[8:]; T=T[8:]
            rows=[]; trows=[]
            for t in range((n-8)//8):
                St=S[8*t:8*t+8]; Tt=T[8*t:8*t+8]
                Z=[full(St[:,8*s+j:8*s+j+1]) for j in range(8)]
                for p in range(0,8,2):
                    for i in range(p+2,8):
                        Z[i]=Z[i]-(E[i,p]*Z[p]+E[i,p+1]*Z[p+1])
                for p in range(0,8,2):
                    Z[p+1]=Z[p+1]-E[p+1,p]*Z[p]
                Z=[z*r for z,r in zip(Z,ra)]
                def dot8(X):
                    m=[z*x for z,x in zip(Z,X)]
                    return ((m[0]+m[1])+(m[2]+m[3]))+((m[4]+m[5])+(m[6]+m[7]))
                rows.append(St-dot8(W)); trows.append(Tt-dot8(V))
            S=jnp.concatenate(rows,0); T=jnp.concatenate(trows,0)
    return jnp.concatenate(U,0), jnp.concatenate(M,0)

def chol_kernel(a_ref, l_ref, m_ref, w_ref, d_ref):
    def blk(i, j):
        return (pl.ds(128 * i, 128), pl.ds(128 * j, 128))

    zero = jnp.zeros((128, 128), jnp.float32)
    for i in range(6):
        for j in range(6):
            if j > i:
                l_ref[blk(i, j)] = zero
                m_ref[blk(i, j)] = zero
                continue
            v = a_ref[blk(i, j)]
            if i // 2 == j // 2:
                v = 0.5 * (v + (v.T if i == j else a_ref[blk(j, i)].T))
            w_ref[blk(i, j)] = v
    tri = lax.broadcasted_iota(jnp.int32, (128, 128), 0) >= lax.broadcasted_iota(jnp.int32, (128, 128), 1)

    def step(k, carry):
        at = pl.multiple_of(k * 128, 128)
        here = (pl.ds(at, 128), pl.ds(at, 128))
        U, M = base(w_ref[here])
        l_ref[here] = jnp.where(tri, U.T, 0.0)
        m_ref[here] = M
        d_ref[...] = M
        for kk in range(6):
            @pl.when(k == kk)
            def _(kk=kk):
                M = d_ref[...]
                if kk < 5:
                    n, r0 = 128 * (5 - kk), 128 * (kk + 1)
                    P = nt(w_ref[pl.ds(r0, n), pl.ds(128 * kk, 128)], M)
                    l_ref[pl.ds(r0, n), pl.ds(128 * kk, 128)] = P
                    for j in range(kk + 1, 6):
                        q0 = 128 * (j - kk - 1)
                        w_ref[pl.ds(128 * j, n - q0), pl.ds(128 * j, 128)] -= nt(P[q0:], P[q0:q0 + 128])
                if kk > 0:
                    acc = nn(l_ref[pl.ds(128 * kk, 128), pl.ds(0, 128 * kk)], m_ref[pl.ds(0, 128 * kk), pl.ds(0, 128 * kk)])
                    m_ref[pl.ds(128 * kk, 128), pl.ds(0, 128 * kk)] = -nn(M, acc)
        return carry

    lax.fori_loop(0, 6, step, 0)


STEPS = (((0, 0, 0), (1, 1, 0)), ((0, 0, 1), (1, 1, 1)), ((0, 1, 0), (1, 0, 0)), ((0, 1, 1), (1, 0, 1)))


def order_offsets():
    def use(o):
        dz, dy, dx, dk = o
        return (dz, dx, int(dy in (1, 2)), int(dy in (2, 3)))

    def even(rest):
        out, load, count = [], [0, 0, 0, 0], len(rest)
        total = [sum(c) for c in zip(*map(use, rest))]
        while rest:
            share = (len(out) + 1) / count
            best = min(rest, key=lambda o: (sum((a + b - t * share) ** 2 for a, b, t in zip(load, use(o), total)), rank[o]))
            rest.remove(best)
            out.append(best)
            load = [a + b for a, b in zip(load, use(best))]
        return out

    every = [(n // 16, (n // 4) % 4, (n // 2) % 2, n % 2) for n in range(1, 32)]
    rank = {o: (o[0] * RANK[0] + o[1] * RANK[1] + o[2] * RANK[2] + o[3] * RANK[3]) % 31 for o in every}
    final = [o for o in every if (o[1] % 2, o[2], o[3]) in STEPS[3]]
    return even([o for o in every if o not in final]), even(list(final))


RANK = (3, 17, 5, 2)
EARLY, LATE = order_offsets()
OFFSETS = (EARLY + LATE, EARLY[::-1] + LATE[::-1])
BATCH = (8, 3, 3, 3)


def spread(w, g, s, col):
    if col == 0:
        return s(0)
    if col == 5:
        return s(3)
    if col == 1:
        return s(1) * w[g, 0:1]
    if col == 2:
        return s(1) * w[g, 1:2] + s(2) * w[g, 2:3]
    if col == 3:
        return s(1) * w[g, 3:4] + s(2) * w[g, 4:5]
    return s(2) * w[g, 5:6]


def front_kernel(rows_ref, cols_ref, child_hbm, base_hbm, res, child, packed, arr, base, lbuf, cbuf, w_in, wb, top, work, low, inv, diag, inv_hi, inv_lo,
                 lsem, ssem, rsem, dsem, wsem, csem, ysem, xsem, ksem):
    pair = lax.axis_index("pair")
    z = lax.axis_index("bit")
    f = lax.axis_index("front")
    y, x, k = f // 4, (f // 2) % 2, f % 2
    me = z * 16 + f

    def at(dz, dy, dx, dk):
        return (pair, (z + dz) % 2, ((y + dy) % 4) * 4 + ((x + dx) % 2) * 2 + (k + dk) % 2)

    child_copy = pltpu.make_async_copy(child_hbm, child, lsem.at[0])
    base_copy = pltpu.make_async_copy(base_hbm.at[0, 0], base, lsem.at[1])
    child_copy.start()
    base_copy.start()
    bar = pltpu.get_barrier_semaphore()
    for n in range(1, 32):
        pl.semaphore_signal(bar, inc=1, device_id=at(n // 16, (n // 4) % 4, (n // 2) % 2, n % 2), device_id_type=MESH)
    pl.semaphore_wait(bar, 31)

    c1, c2 = cols_ref[0, 1], cols_ref[0, 2]
    lines = [jnp.broadcast_to(jnp.where(c, 1.0, 0.0), (1, 128)) for c in (c1 == 1, c1 == 2, c2 == 2, c1 == 3, c2 == 3, c2 == 4)]
    masks = jnp.concatenate(lines + [jnp.zeros((2, 128), jnp.float32)], 0)
    w_in[...] = masks
    wb[z] = masks
    wcopy = pltpu.make_async_remote_copy(
        src_ref=w_in, dst_ref=wb.at[z], send_sem=wsem.at[0], recv_sem=wsem.at[1],
        device_id=at(1, 0, 0, 0), device_id_type=MESH)
    wcopy.start()
    child_copy.wait()

    def tile_for(d):
        target = 32 * (f % 8) + 2 * (d % 16) + d // 16
        i = jnp.int32(0)
        for t in range(14):
            i = jnp.where(rows_ref[t] == target, t + 1, i)
        return jnp.where(i > 0, child[jnp.maximum(i - 1, 0)], 0.0)

    source = (f == 0) | (f == 8)
    half = z * 2 + y // 2
    widths = (256, 384, 512)

    def child_send(b, q):
        n = widths[q]
        return pltpu.make_async_remote_copy(
            src_ref=lbuf.at[3 * b + q, :, pl.ds(0, n)], dst_ref=cbuf.at[half, :, pl.ds(0, n)], send_sem=dsem.at[b * 3 + q],
            recv_sem=csem.at[half], device_id=(pair, b, q), device_id_type=MESH)

    def own(b, q):
        return (f == q) & (z == b)

    @pl.when(source)
    def _():
        for q in (2, 1, 0):
            for b in range(2):
                lbuf[3 * b + q] = tile_for(16 * b + q)

                @pl.when(jnp.logical_not(own(b, q)))
                def _(b=b, q=q):
                    child_send(b, q).start()

    def offset(n):
        a, b = OFFSETS[0][n], OFFSETS[1][n]
        return tuple(u + k * (v - u) for u, v in zip(a, b))

    def bulk(n):
        dz, dy, dx, dk = offset(n)
        to = at(dz, dy, dx, dk)
        return to, pltpu.make_async_remote_copy(
            src_ref=packed.at[n], dst_ref=arr.at[me], send_sem=ssem.at[n], recv_sem=rsem.at[me], device_id=to, device_id_type=MESH)

    def batch(lo, hi):
        for n in range(lo, hi):
            to, copy = bulk(n)
            packed[n] = tile_for(to[1] * 16 + to[2])
            copy.start()

    marks = [sum(BATCH[:i]) for i in range(5)]
    batch(0, marks[1])
    arr[me] = tile_for(me)
    base_copy.wait()
    wcopy.wait_recv()

    for q in range(3):
        n = widths[q]

        @pl.when(f == q)
        def _(q=q, n=n):
            for s in range(4):
                mine_too = (f == 0) & (half == s)

                @pl.when(jnp.logical_not(mine_too))
                def _(s=s):
                    pltpu.make_async_remote_copy(
                        src_ref=lbuf.at[0, :, pl.ds(0, n)], dst_ref=cbuf.at[s, :, pl.ds(0, n)], send_sem=dsem.at[0],
                        recv_sem=csem.at[s], device_id=at(1, 0, 0, 0), device_id_type=MESH).wait_recv()

                if q == 0:
                    @pl.when(mine_too)
                    def _(s=s):
                        cbuf[s, :, 0:256] = lbuf[3 * z, :, 0:256]
            row = pl.ds(pl.multiple_of((2 * q + z) * 128, 128), 128)
            for col in range(2 * q + 2):
                v = base[0, :, 128 * col:128 * col + 128]
                for g in range(2):
                    v = v + spread(wb, g, lambda c, g=g: cbuf[2 * g, :, 128 * c:128 * c + 128] + cbuf[2 * g + 1, :, 128 * c:128 * c + 128], col)
                top[row, 128 * col:128 * col + 128] = v

    def tile_copy(q, zz, send, recv, to):
        piece = top.at[pl.ds(pl.multiple_of((2 * q + zz) * 128, 128), 128), pl.ds(0, 256 * q + 256)]
        return pltpu.make_async_remote_copy(
            src_ref=piece, dst_ref=piece, send_sem=send, recv_sem=recv, device_id=to, device_id_type=MESH)

    mine = f % 4
    for q in range(3):
        @pl.when(f == q)
        def _(q=q):
            for n, dy in enumerate((2, 1, 3)):
                tile_copy(q, z, dsem.at[6 + n], ysem.at[0], at(0, dy, 0, 0)).start()
    batch(marks[1], marks[2])
    for q in range(3):
        @pl.when(mine == q)
        def _(q=q):
            @pl.when(y > 0)
            def _():
                tile_copy(q, z, dsem.at[6], ysem.at[0], at(0, 1, 0, 0)).wait_recv()

            for n, (dz, dx) in enumerate(((1, 1), (0, 1), (1, 0))):
                tile_copy(q, z, dsem.at[9 + n], xsem.at[2 * q + z], at(dz, 0, dx, 0)).start()
            tile_copy(q, z, dsem.at[(14 if q == 2 else 12) + z], ksem.at[2 * q + z], at(0, 0, 0, 1)).start()
    batch(marks[2], marks[3])
    for q in range(3):
        @pl.when(k == q % 2)
        def _(q=q):
            for zz in range(2):
                @pl.when((mine != q) | (z != zz))
                def _(zz=zz):
                    tile_copy(q, zz, dsem.at[9], xsem.at[2 * q + zz], at(0, 0, 1, 0)).wait_recv()
                    tile_copy(q, zz, dsem.at[(14 if q == 2 else 12) + zz], ksem.at[2 * q + zz], at(0, 0, 0, 1)).start()
    batch(marks[3], marks[4])
    for q in range(3):
        @pl.when(k != q % 2)
        def _(q=q):
            for zz in range(2):
                tile_copy(q, zz, dsem.at[9], ksem.at[2 * q + zz], at(0, 0, 0, 1)).wait_recv()
    batch(marks[4], 31)

    chol_kernel(top, low, inv, work, diag)
    v = inv[...]
    hi = v.astype(jnp.bfloat16)
    inv_hi[...] = hi
    inv_lo[...] = (v - hi.astype(jnp.float32)).astype(jnp.bfloat16)

    def slot_of(e):
        ey, ex, ek = STEPS[e // 2][e % 2]
        return ((y + ey) % 2) * 4 + ((x + ex) % 2) * 2 + (k + ek) % 2

    for step in range(4):
        rows = []
        for e in (2 * step, 2 * step + 1):
            j = slot_of(e)
            for g in range(2):
                for h in range(2):
                    src = g * 16 + h * 8 + j

                    @pl.when(src != me)
                    def _(src=src):
                        pltpu.make_async_remote_copy(
                            src_ref=packed.at[0], dst_ref=arr.at[src], send_sem=ssem.at[0], recv_sem=rsem.at[src],
                            device_id=at(1, 0, 0, 0), device_id_type=MESH).wait_recv()
            cols = []
            for col in range(6):
                v = base[j, :, 128 * col:128 * col + 128]
                for g in range(2):
                    v = v + spread(wb, g, lambda c, g=g: arr[g * 16 + j, :, 128 * c:128 * c + 128] + arr[g * 16 + 8 + j, :, 128 * c:128 * c + 128], col)
                cols.append(v)
            rows.append(jnp.concatenate(cols, 1))
        a = jnp.concatenate(rows, 0)
        a_hi = a.astype(jnp.bfloat16)
        a_lo = (a - a_hi.astype(jnp.float32)).astype(jnp.bfloat16)
        for s in range(3):
            n = 256 * s + 256
            m_hi, m_lo = inv_hi[n - 256:n, :n], inv_lo[n - 256:n, :n]
            v = (nt(a_lo[:, :n], m_hi, None) + nt(a_hi[:, :n], m_lo, None)) + nt(a_hi[:, :n], m_hi, None)
            for e in (0, 1):
                res[0, 0, slot_of(2 * step + e), :, n - 256:n] = v[128 * e:128 * e + 128]
        for e in (2 * step, 2 * step + 1):
            @pl.when((slot_of(e) == 0) & (f <= 2))
            def _(e=e):
                res[0, 0, 0] = low[pl.ds(pl.multiple_of((2 * f + z) * 128, 128), 128), :]

    for n in range(31):
        bulk(n)[1].wait_send()
    wcopy.wait_send()

    @pl.when(source)
    def _():
        for q in range(3):
            for b in range(2):
                @pl.when(jnp.logical_not(own(b, q)))
                def _(b=b, q=q):
                    child_send(b, q).wait_send()

    for q in range(3):
        @pl.when(f == q)
        def _(q=q):
            for n in range(3):
                tile_copy(q, z, dsem.at[6 + n], ysem.at[0], at(0, 1, 0, 0)).wait_send()

        @pl.when(mine == q)
        def _(q=q):
            for n in range(3):
                tile_copy(q, z, dsem.at[9 + n], xsem.at[2 * q + z], at(0, 0, 1, 0)).wait_send()

        @pl.when(k == q % 2)
        def _(q=q):
            for zz in range(2):
                tile_copy(q, zz, dsem.at[(14 if q == 2 else 12) + zz], ksem.at[2 * q + zz], at(0, 0, 0, 1)).wait_send()


def fronts(rows, cols, tiles, base_tiles):
    f32 = jnp.float32
    square = pltpu.VMEM((768, 768), f32)
    dma = pltpu.SemaphoreType.DMA
    return pl.pallas_call(
        front_kernel,
        out_shape=jax.ShapeDtypeStruct((1, 1, 8, 128, 768), f32),
        in_specs=[SM, SM, ANY, ANY],
        out_specs=VM,
        scratch_shapes=[
            pltpu.VMEM((14, 128, 512), f32),
            pltpu.VMEM((31, 128, 512), f32),
            pltpu.VMEM((32, 128, 512), f32),
            pltpu.VMEM((8, 128, 768), f32),
            pltpu.VMEM((6, 128, 512), f32),
            pltpu.VMEM((4, 128, 512), f32),
            pltpu.VMEM((8, 128), f32),
            pltpu.VMEM((2, 8, 128), f32),
            square, square, square, square,
            pltpu.VMEM((128, 128), f32),
            pltpu.VMEM((768, 768), jnp.bfloat16),
            pltpu.VMEM((768, 768), jnp.bfloat16),
            dma((2,)), dma((31,)), dma((32,)), dma((16,)), dma((2,)), dma((4,)), dma((1,)), dma((6,)), dma((6,)),
        ],
        compiler_params=pltpu.CompilerParams(collective_id=0, has_side_effects=True, vmem_limit_bytes=46 << 20),
        name="fronts",
    )(rows, cols, tiles, base_tiles)


def body(child_block, child_rows, child_cols, parent_base):
    return fronts(child_rows[0, 0], child_cols, child_block[0, 0], parent_base)


def solution(mesh):
    mesh = Mesh(mesh.devices.reshape(4, 2, 16), ("pair", "bit", "front"))
    cube = ("pair", "bit")
    placed = (P(cube, "front"), P(cube, "front"), P(cube), P(cube, "front"))
    return jax.shard_map(body, mesh=mesh, in_specs=placed, out_specs=P(cube, "front"), check_vma=False)
```
